512 devices in a mesh: row: 8 (over x, core), col: 64 (over y, z).
Axes of the slice: x: 4, y: 4, z: 16, core: 2. Of those that a mesh axis runs over, the one named last changes fastest.
Arguments:
- diag_factors: bfloat16 [3, 512, 512], replicated, as said below
- panel_v: bfloat16 [64, 2, 512, 128], P('row', None, 'col'), may hold values from -2.515625 to 2.515625
- ranks: int32 [64, 2], P('row'), may hold values from 32 to 128, as said below
Outputs:
- panel_factors: bfloat16 [64, 1024, 256], P('row', 'col')
- update_cores: float32 [64, 64, 256, 256], P('row', 'col')
The draws below stay inside these ranges and needn't reach their ends.
Inputs may be any that keep to these rules, and one draw needn't show every extreme that they name: `ranks`: every panel tile has rank at least 32; the tiles of array row 0 have rank 128. `diag_factors`: inverse0 and inverse1 are lower triangular with positive diagonals.
All inputs are finite; a program needn't handle non-finite values.
Results may differ from the reference program's by a relative error of at most 0.0046.
Values may be sent and summed in bfloat16 or wider, within the bound.
No kernel may reach another device: no remote copies, remote signals or barrier semaphores. Data moves between devices by JAX's collectives and lax.ppermute only.
A program may use at most 64 MiB of HBM per device.

```python
import jax
import jax.numpy as jnp
from jax import lax

NB = 512
RMAX = 128
R_DEV = 8
NTR = 64
NTC = 64
N_ROW = 8


def draw_diag_factors(key, part):
    key = jax.random.fold_in(key, 11)
    k1, k2, k3 = jax.random.split(key, 3)
    noise = jax.random.normal(k1, (3, NB, NB), jnp.float32)
    rows = jnp.arange(NB, dtype=jnp.int32)
    below = (rows[:, None] > rows[None, :]).astype(jnp.float32)
    ident = (rows[:, None] == rows[None, :]).astype(jnp.float32)
    scale = 1.0 / jnp.sqrt(jnp.float32(NB))
    d0 = jnp.exp(jax.random.uniform(k2, (NB,), jnp.float32, jnp.log(0.45), jnp.log(0.63)))
    d1 = jnp.exp(jax.random.uniform(k3, (NB,), jnp.float32, jnp.log(0.45), jnp.log(0.63)))
    inverse0 = noise[0] * below * (0.3 * scale) + ident * d0[:, None]
    couple = noise[1] * (0.5 * scale)
    inverse1 = noise[2] * below * (0.3 * scale) + ident * d1[:, None]
    return jnp.stack([inverse0, couple, inverse1]).astype(jnp.bfloat16)


def draw_ranks(key, part):
    key = jax.random.fold_in(key, 23)
    drawn = jax.random.randint(key, (NTR, 2), RMAX // 4, RMAX + 1, dtype=jnp.int32)
    return drawn.at[0].set(RMAX)


def steps_of(stream_key, extent, pieces, least, largest):
    def one(axis_at, parts):
        draws = jax.random.uniform(jax.random.fold_in(jax.random.fold_in(stream_key, 6), axis_at), (parts,), jnp.float32, least / len(pieces), largest / len(pieces))
        return jnp.repeat(jnp.exp(draws), extent[axis_at] // parts).reshape((-1,) + (1,) * (len(extent) - axis_at - 1))

    factor_of = one(*pieces[0])
    for cut in pieces[1:]:
        factor_of = factor_of * one(*cut)
    return factor_of


def bell_draw(key, extent, scale, limit, pieces=(), held_as=jnp.bfloat16):
    factor_of = steps_of(key, extent, pieces, -0.22, 0.18) if pieces else 1.0
    values = jax.random.normal(key, extent, jnp.float32) * scale * factor_of
    return jnp.minimum(jnp.maximum(values, -limit), limit).astype(held_as)


def setup_inputs(seed: int = 0) -> dict:
    arg_keys = jax.random.split(jax.random.key(seed), 4)
    return {
        "diag_factors": draw_diag_factors(jax.random.fold_in(arg_keys[3], 71), 0),
        "panel_v": bell_draw(arg_keys[1], (NTR, 2, NB, RMAX), (2.0 * NB ** -0.25), 2.515625, ((0, 8), (2, 64))),
        "ranks": draw_ranks(jax.random.fold_in(arg_keys[3], 71), 0),
    }


def assemble(w_block, lower, right):
    top = jnp.concatenate([w_block, jnp.zeros_like(w_block)], axis=-1)
    bottom = jnp.concatenate([lower, right], axis=-1)
    return jnp.concatenate([top, bottom], axis=-2)


def reference(diag_factors, panel_v, ranks):
    high = lax.Precision.HIGHEST
    inverse0 = diag_factors[0]
    couple = diag_factors[1]
    inverse1 = diag_factors[2]
    columns = jnp.arange(RMAX, dtype=jnp.int32)
    keep = columns[None, None, :] < ranks[:, :, None]
    masked = jnp.where(keep[:, :, None, :], panel_v, jnp.zeros_like(panel_v))
    m32 = masked.astype(jnp.float32)
    w_block = jnp.einsum('nm,tmr->tnr', inverse0.astype(jnp.float32), m32[:, 0], precision=high).astype(jnp.bfloat16)
    lower = jnp.einsum('nm,tmr->tnr', couple.astype(jnp.float32), w_block.astype(jnp.float32), precision=high).astype(jnp.bfloat16)
    right = jnp.einsum('nm,tmr->tnr', inverse1.astype(jnp.float32), m32[:, 1], precision=high).astype(jnp.bfloat16)
    factors = assemble(w_block, lower, right)
    slab = jnp.arange(NTC, dtype=jnp.int32)
    owner_rows = (slab % N_ROW) * R_DEV + slab // N_ROW
    tile_rows = jnp.arange(NTR, dtype=jnp.int32)
    codes = (tile_rows % R_DEV) * N_ROW + tile_rows // R_DEV
    f32 = factors.astype(jnp.float32)
    chosen = f32[owner_rows]
    cores = jnp.einsum('akr,bks->abrs', f32, chosen, precision=high)
    active = codes[:, None] > slab[None, :]
    cores = jnp.where(active[:, :, None, None], cores, jnp.zeros_like(cores))
    return factors, cores
```

```python
import jax
import jax.numpy as jnp
from jax import lax
from jax.sharding import PartitionSpec as P

Y = 4
Z = 16


def dot(a, b, dims):
    return lax.dot_general(a, b, (dims, ((), ())), preferred_element_type=jnp.float32)


def shards(diag_factors, panel_v, ranks):
    tiles, pair, mine, rank = panel_v.shape
    nrow = lax.axis_size("row")
    prow = lax.axis_index("row")
    qcol = lax.axis_index("col")
    bf16 = jnp.bfloat16
    along_z = [[y * Z + z for z in range(Z)] for y in range(Y)]
    along_y = [[y * Z + z for y in range(Y)] for z in range(Z)]
    flat = panel_v.transpose(2, 0, 1, 3).reshape(mine, tiles * pair * rank)
    keep = jnp.arange(rank, dtype=jnp.int32)[None, None, :] < ranks[:, :, None]
    flat = jnp.where(keep.reshape(1, -1), flat, jnp.zeros_like(flat))
    slab = lax.all_gather(flat, "col", axis=0, tiled=True, axis_index_groups=along_z)
    sent = jnp.broadcast_to(slab[None], (Y,) + slab.shape)
    whole = lax.all_to_all(sent, "col", 0, 0, axis_index_groups=along_y)
    whole = whole.reshape(-1, flat.shape[1])
    nloc = whole.shape[0]
    wide = pair * rank
    picked = lax.dynamic_slice_in_dim(whole, (qcol // nrow) * wide, wide, 1)
    cut = lax.all_to_all(picked.reshape(nrow, nloc // nrow, wide), "row", 0, 0)
    cut = lax.dynamic_index_in_dim(cut, qcol % nrow, 0, keepdims=True)
    column = lax.all_to_all(jnp.broadcast_to(cut, (nrow,) + cut.shape[1:]), "row", 0, 0)
    column = column.reshape(nloc, wide)

    def factor(v):
        v = v.reshape(nloc, -1, pair, rank)
        w = dot(diag_factors[0], v[:, :, 0].reshape(nloc, -1), ((1,), (0,))).astype(bf16)
        right = dot(diag_factors[2], v[:, :, 1].reshape(nloc, -1), ((1,), (0,))).astype(bf16)
        lower = dot(diag_factors[1], w, ((1,), (0,))).astype(bf16)
        w, lower, right = (a.reshape(nloc, -1, 1, rank) for a in (w, lower, right))
        top = jnp.concatenate([w, jnp.zeros_like(w)], 2)
        bottom = jnp.concatenate([lower, right], 2)
        return jnp.concatenate([top, bottom], 0).reshape(2 * nloc, -1, wide)

    factors = factor(whole)
    mate = factor(column)[:, 0]
    piece = 2 * nloc // lax.axis_size("col")
    share = lax.dynamic_slice_in_dim(factors, qcol * piece, piece, 0).transpose(1, 0, 2)
    cores = jnp.einsum("ktr,ks->trs", factors, mate, preferred_element_type=jnp.float32)
    codes = jnp.arange(tiles, dtype=jnp.int32) * nrow + prow
    cores = jnp.where((codes > qcol)[:, None, None], cores, jnp.zeros_like(cores))
    return share, cores[:, None]


def solution(mesh):
    placed = (P(), P("row", None, "col", None), P("row", None))
    return jax.shard_map(
        shards,
        mesh=mesh,
        in_specs=placed,
        out_specs=(P("row", "col", None), P("row", "col", None, None)),
        check_vma=False,
    )
```

```python
import jax
import jax.numpy as jnp
from jax import lax
from jax.experimental import pallas as pl
from jax.experimental.pallas import tpu as pltpu
from jax.sharding import PartitionSpec as P

Y = 4
Z = 16
BF16 = jnp.bfloat16


def dot(a, b, ca, cb):
    return lax.dot_general(a, b, (((ca,), (cb,)), ((), ())), preferred_element_type=jnp.float32)


def own_factors(place, ranks, diag, v, wt, lt, rt, share):
    step = pl.program_id(0)
    piece = share.shape[1]
    nloc = v.shape[0]
    rank = v.shape[1] // 4
    q = place[0]
    half = nloc // piece
    rows = pl.ds(pl.multiple_of(lax.rem(q, half) * piece, piece), piece)
    first = q < half
    row = lax.broadcasted_iota(jnp.int32, (2 * rank, 1), 0)
    lane = lax.broadcasted_iota(jnp.int32, (1, 2 * rank), 1)

    def keep(at, k):
        one, two = ranks[4 * step + k], ranks[4 * step + 2 + k]
        return at < jnp.where(at < rank, one, two + rank)

    block = v[...]
    v0 = jnp.concatenate([block[:, :rank], block[:, 2 * rank : 3 * rank]], 1)
    v1 = jnp.concatenate([block[:, rank : 2 * rank], block[:, 3 * rank :]], 1)
    w = dot(v0, diag[0], 0, 1)
    w = jnp.where(keep(row, 0), w, 0.0).astype(BF16)
    wt[...] = w
    lt[...] = dot(w, diag[1], 1, 1).astype(BF16)
    r = dot(v1, diag[2], 0, 1)
    rt[...] = jnp.where(keep(row, 1), r, 0.0).astype(BF16)
    top = jnp.where(keep(lane, 0), dot(diag[0, rows, :], v0, 1, 0), 0.0)
    low = dot(diag[1, rows, :], w, 1, 1)
    side = jnp.where(keep(lane, 1), dot(diag[2, rows, :], v1, 1, 0), 0.0)
    left = jnp.where(first, top, low).astype(BF16)
    right = jnp.where(first, 0.0, side).astype(BF16)
    for t in range(2):
        cut = slice(t * rank, (t + 1) * rank)
        share[t, :, :rank] = left[:, cut]
        share[t, :, rank:] = right[:, cut]


def tile_cores(place, diag, column, wt, lt, rt, cores, wc, lrc):
    step = pl.program_id(0)
    rank = wc.shape[1]

    @pl.when(step == 0)
    def _():
        w = dot(diag[0], column[:, :rank], 1, 0).astype(BF16)
        wc[...] = w
        lrc[:, :rank] = dot(diag[1], w, 1, 0).astype(BF16)
        lrc[:, rank:] = dot(diag[2], column[:, rank:], 1, 0).astype(BF16)

    both = dot(lt[...], lrc[...], 1, 0)
    corner = dot(wt[...], wc[...], 1, 0)
    below = dot(rt[...], lrc[...], 1, 0)
    for t in range(2):
        cut = slice(t * rank, (t + 1) * rank)
        active = (2 * step + t) * place[2] + place[1] > place[0]
        cores[t, :rank, :rank] = jnp.where(active, both[cut, :rank] + corner[cut], 0.0)
        cores[t, :rank, rank:] = jnp.where(active, both[cut, rank:], 0.0)
        cores[t, rank:, :] = jnp.where(active, below[cut], 0.0)


def shards(diag_factors, panel_v, ranks):
    tiles, pair, mine, rank = panel_v.shape
    nrow = lax.axis_size("row")
    ncol = lax.axis_size("col")
    prow = lax.axis_index("row")
    qcol = lax.axis_index("col")
    along_z = [[y * Z + z for z in range(Z)] for y in range(Y)]
    along_y = [[y * Z + z for y in range(Y)] for z in range(Z)]
    wide = pair * rank
    place = jnp.stack([qcol, prow, jnp.int32(nrow)]).astype(jnp.int32)
    flat = panel_v.transpose(2, 0, 1, 3).reshape(mine, tiles * wide)
    slab = lax.all_gather(flat, "col", axis=0, tiled=True, axis_index_groups=along_z)
    sent = jnp.broadcast_to(slab[None], (Y,) + slab.shape)
    whole = lax.all_to_all(sent, "col", 0, 0, axis_index_groups=along_y)
    whole = whole.reshape(-1, flat.shape[1])
    nloc = whole.shape[0]
    local_row = qcol // nrow
    picked = lax.dynamic_slice_in_dim(whole, local_row * wide, wide, 1)
    limit = lax.dynamic_index_in_dim(ranks, local_row, 0, keepdims=False)
    at = jnp.arange(wide, dtype=jnp.int32)
    keep = jnp.where(at < rank, at < limit[0], at < limit[1] + rank)
    picked = jnp.where(keep[None], picked, jnp.zeros_like(picked))
    cut = lax.all_to_all(picked.reshape(nrow, nloc // nrow, wide), "row", 0, 0)
    cut = lax.dynamic_index_in_dim(cut, qcol % nrow, 0, keepdims=True)
    column = lax.all_to_all(jnp.broadcast_to(cut, (nrow,) + cut.shape[1:]), "row", 0, 0)
    column = column.reshape(nloc, wide)

    steps = tiles // 2
    scalars = pl.BlockSpec(memory_space=pltpu.SMEM)
    matrices = pl.BlockSpec(diag_factors.shape, lambda i: (0, 0, 0))
    turned = pl.BlockSpec((wide, nloc), lambda i: (i, 0))
    lying = jax.ShapeDtypeStruct((tiles * rank, nloc), BF16)
    piece = 2 * nloc // ncol
    limits = pltpu.CompilerParams(vmem_limit_bytes=32 << 20)
    wt, lt, rt, share = pl.pallas_call(
        own_factors,
        grid=(steps,),
        in_specs=[scalars, scalars, matrices, pl.BlockSpec((nloc, 2 * wide), lambda i: (0, i))],
        out_specs=[turned] * 3 + [pl.BlockSpec((2, piece, wide), lambda i: (i, 0, 0))],
        out_shape=[lying] * 3 + [jax.ShapeDtypeStruct((tiles, piece, wide), BF16)],
        compiler_params=limits,
        cost_estimate=pl.CostEstimate(flops=8 * 10**9, bytes_accessed=8 << 20, transcendentals=0),
        name="own_factors",
    )(place, ranks.reshape(-1), diag_factors, whole)
    cores = pl.pallas_call(
        tile_cores,
        grid=(steps,),
        in_specs=[scalars, matrices, pl.BlockSpec((nloc, wide), lambda i: (0, 0))] + [turned] * 3,
        out_specs=pl.BlockSpec((2, wide, wide), lambda i: (i, 0, 0)),
        out_shape=jax.ShapeDtypeStruct((tiles, wide, wide), jnp.float32),
        scratch_shapes=[pltpu.VMEM((nloc, rank), BF16), pltpu.VMEM((nloc, wide), BF16)],
        compiler_params=limits,
        cost_estimate=pl.CostEstimate(flops=2 * 10**9, bytes_accessed=7 << 20, transcendentals=0),
        name="tile_cores",
    )(place, diag_factors, column, wt, lt, rt)
    return share, cores[:, None]


def solution(mesh):
    placed = (P(), P("row", None, "col", None), P("row", None))
    return jax.shard_map(
        shards,
        mesh=mesh,
        in_specs=placed,
        out_specs=(P("row", "col", None), P("row", "col", None, None)),
        check_vma=False,
    )
```

```python
import jax
import jax.numpy as jnp
from jax import lax
from jax.experimental import pallas as pl
from jax.experimental.pallas import tpu as pltpu
from jax.sharding import PartitionSpec as P

Y = 4
Z = 16
BF16 = jnp.bfloat16


def dot(a, b, ca, cb):
    return lax.dot_general(a, b, (((ca,), (cb,)), ((), ())), preferred_element_type=jnp.float32)


def pick_tiles(place, ranks, ta, tb, tc, td, picked):
    rank = picked.shape[3] // 2
    lane = lax.broadcasted_iota(jnp.int32, (1, 2 * rank), 1)
    for y, tile in enumerate((ta, tb, tc, td)):
        at = place[4 + y]
        keep = lane < jnp.where(lane < rank, ranks[0, at], ranks[1, at] + rank)
        kept = jnp.where(keep, tile[...].astype(jnp.float32), 0.0).astype(BF16)
        picked[:, y] = kept.reshape(picked.shape[0], picked.shape[2], picked.shape[3])


def own_factors(place, ranks, diag, va, vb, vc, vd, wt, lt, rt, share, block):
    step = pl.program_id(0)
    piece = share.shape[1]
    nloc, rank = block.shape[0], block.shape[1] // 4
    part = nloc // Y
    q = place[0]
    half = nloc // piece
    rows = pl.ds(pl.multiple_of(lax.rem(q, half) * piece, piece), piece)
    first = q < half
    row = lax.broadcasted_iota(jnp.int32, (2 * rank, 1), 0)
    lane = lax.broadcasted_iota(jnp.int32, (1, 2 * rank), 1)

    def keep(at, k):
        one, two = ranks[k, 2 * step], ranks[k, 2 * step + 1]
        return at < jnp.where(at < rank, one, two + rank)

    for d, v in enumerate((va, vb, vc, vd)):
        source = lax.rem(place[3] + Y - d, Y)
        block[pl.ds(pl.multiple_of(source * part, part), part), :] = v[...]
    v0 = jnp.concatenate([block[:, :rank], block[:, 2 * rank : 3 * rank]], 1)
    v1 = jnp.concatenate([block[:, rank : 2 * rank], block[:, 3 * rank :]], 1)
    w = dot(v0, diag[0], 0, 1)
    w = jnp.where(keep(row, 0), w, 0.0).astype(BF16)
    wt[...] = w
    lt[...] = dot(w, diag[1], 1, 1).astype(BF16)
    r = dot(v1, diag[2], 0, 1)
    rt[...] = jnp.where(keep(row, 1), r, 0.0).astype(BF16)
    top = jnp.where(keep(lane, 0), dot(diag[0, rows, :], v0, 1, 0), 0.0)
    low = dot(diag[1, rows, :], w, 1, 1)
    side = jnp.where(keep(lane, 1), dot(diag[2, rows, :], v1, 1, 0), 0.0)
    left = jnp.where(first, top, low).astype(BF16)
    right = jnp.where(first, 0.0, side).astype(BF16)
    for t in range(2):
        cut = slice(t * rank, (t + 1) * rank)
        share[t, :, :rank] = left[:, cut]
        share[t, :, rank:] = right[:, cut]


def tile_cores(place, diag, cuts, wt, lt, rt, cores, column, wc, lrc):
    step = pl.program_id(0)
    rank = wc.shape[1]

    @pl.when(step == 0)
    def _():
        rows = cuts.shape[1] // Y
        for y in range(Y):
            for p in range(cuts.shape[0]):
                at = (y * cuts.shape[0] + p) * rows
                column[at : at + rows, :] = cuts[p, y * rows : (y + 1) * rows, :]
        w = dot(diag[0], column[:, :rank], 1, 0).astype(BF16)
        wc[...] = w
        lrc[:, :rank] = dot(diag[1], w, 1, 0).astype(BF16)
        lrc[:, rank:] = dot(diag[2], column[:, rank:], 1, 0).astype(BF16)

    both = dot(lt[...], lrc[...], 1, 0)
    corner = dot(wt[...], wc[...], 1, 0)
    below = dot(rt[...], lrc[...], 1, 0)
    for t in range(2):
        cut = slice(t * rank, (t + 1) * rank)
        active = (2 * step + t) * place[2] + place[1] > place[0]
        cores[t, :rank, :rank] = jnp.where(active, both[cut, :rank] + corner[cut], 0.0)
        cores[t, :rank, rank:] = jnp.where(active, both[cut, rank:], 0.0)
        cores[t, rank:, :] = jnp.where(active, below[cut], 0.0)


def shards(diag_factors, panel_v, ranks):
    tiles, pair, mine, rank = panel_v.shape
    nrow = lax.axis_size("row")
    ncol = lax.axis_size("col")
    prow = lax.axis_index("row")
    qcol = lax.axis_index("col")
    along_z = [[y * Z + z for z in range(Z)] for y in range(Y)]
    across = [[(p * Y + y) * Z + z for p in range(nrow) for y in range(Y)] for z in range(Z)]
    wide = pair * rank
    ycol, zcol = qcol // Z, qcol % Z
    local = [(y * Z + zcol) // nrow for y in range(Y)]
    place = jnp.stack([qcol, prow, jnp.int32(nrow), ycol] + local).astype(jnp.int32)
    flat = panel_v.transpose(2, 0, 1, 3).reshape(mine, tiles * wide)
    slab = lax.all_gather(flat, "col", axis=0, tiled=True, axis_index_groups=along_z)
    parts = [slab] + [
        lax.ppermute(slab, "col", [(y * Z + z, (y + d) % Y * Z + z) for y in range(Y) for z in range(Z)])
        for d in range(1, Y)
    ]
    nloc = Y * slab.shape[0]
    rows = slab.shape[0] // nrow

    def of(y):
        return pl.BlockSpec((slab.shape[0], wide), lambda i, where: (0, where[4 + y]))

    picked = pl.pallas_call(
        pick_tiles,
        grid_spec=pltpu.PrefetchScalarGridSpec(
            num_scalar_prefetch=1,
            grid=(1,),
            in_specs=[pl.BlockSpec(memory_space=pltpu.SMEM)] + [of(y) for y in range(Y)],
            out_specs=pl.BlockSpec((nrow, Y, rows, wide), lambda i, where: (0, 0, 0, 0)),
        ),
        out_shape=jax.ShapeDtypeStruct((nrow, Y, rows, wide), BF16),
        compiler_params=pltpu.CompilerParams(vmem_limit_bytes=4 << 20),
        name="pick_tiles",
    )(place, ranks.T, *[slab] * Y)
    picked = picked.reshape(nrow * Y, rows, wide)
    cut = lax.all_to_all(picked, ("row", "col"), 0, 0, axis_index_groups=across)
    cut = lax.dynamic_slice_in_dim(cut, zcol % nrow * Y, Y, 0).reshape(1, Y * rows, wide)
    cuts = lax.all_to_all(jnp.broadcast_to(cut, (nrow,) + cut.shape[1:]), "row", 0, 0)

    steps = tiles // 2
    scalars = pl.BlockSpec(memory_space=pltpu.SMEM)
    matrices = pl.BlockSpec(diag_factors.shape, lambda i: (0, 0, 0))
    turned = pl.BlockSpec((wide, nloc), lambda i: (i, 0))
    lying = pltpu.HBM((tiles * rank, nloc), BF16)
    piece = 2 * nloc // ncol
    limits = pltpu.CompilerParams(vmem_limit_bytes=16 << 20)
    wt, lt, rt, share = pl.pallas_call(
        own_factors,
        grid=(steps,),
        in_specs=[scalars, scalars, matrices] + [pl.BlockSpec((nloc // Y, 2 * wide), lambda i: (0, i))] * Y,
        out_specs=[turned] * 3 + [pl.BlockSpec((2, piece, wide), lambda i: (i, 0, 0))],
        out_shape=[lying] * 3 + [jax.ShapeDtypeStruct((tiles, piece, wide), BF16)],
        scratch_shapes=[pltpu.VMEM((nloc, 2 * wide), BF16)],
        compiler_params=limits,
        cost_estimate=pl.CostEstimate(flops=8 * 10**9, bytes_accessed=8 << 20, transcendentals=0),
        name="own_factors",
    )(place, ranks.T, diag_factors, *parts)
    cores = pl.pallas_call(
        tile_cores,
        grid=(steps,),
        in_specs=[scalars, matrices, pl.BlockSpec(cuts.shape, lambda i: (0, 0, 0))] + [turned] * 3,
        out_specs=pl.BlockSpec((2, wide, wide), lambda i: (i, 0, 0)),
        out_shape=jax.ShapeDtypeStruct((tiles, wide, wide), jnp.float32),
        scratch_shapes=[pltpu.VMEM((nloc, n), BF16) for n in (wide, rank, wide)],
        compiler_params=limits,
        cost_estimate=pl.CostEstimate(flops=2 * 10**9, bytes_accessed=7 << 20, transcendentals=0),
        name="tile_cores",
    )(place, diag_factors, cuts, *[pltpu.with_memory_space_constraint(a, pltpu.HBM) for a in (wt, lt, rt)])
    return share, cores[:, None]


def solution(mesh):
    placed = (P(), P("row", None, "col", None), P("row", None))
    return jax.shard_map(
        shards,
        mesh=mesh,
        in_specs=placed,
        out_specs=(P("row", "col", None), P("row", "col", None, None)),
        check_vma=False,
    )
```

```python
import jax
import jax.numpy as jnp
from jax import lax
from jax.experimental import pallas as pl
from jax.experimental.pallas import tpu as pltpu
from jax.sharding import PartitionSpec as P

Y = 4
Z = 16
BF16 = jnp.bfloat16


def dot(a, b, ca, cb):
    return lax.dot_general(a, b, (((ca,), (cb,)), ((), ())), preferred_element_type=jnp.float32)


def pick_tiles(place, ranks, ta, tb, tc, td, picked):
    rank = picked.shape[3] // 2
    lane = lax.broadcasted_iota(jnp.int32, (1, 2 * rank), 1)
    for y, tile in enumerate((ta, tb, tc, td)):
        at = place[4 + y]
        keep = lane < jnp.where(lane < rank, ranks[0, at], ranks[1, at] + rank)
        kept = jnp.where(keep, tile[...].astype(jnp.float32), 0.0).astype(BF16)
        picked[:, y] = kept.reshape(picked.shape[0], picked.shape[2], picked.shape[3])


def spread_cut(place, cut, sent):
    for p in range(sent.shape[0]):
        sent[p] = cut[...]


def own_factors(place, ranks, diag, va, vb, vc, vd, wt, lt, rt, share, block):
    tiles, piece, wide = share.shape
    nloc, rank = block.shape[0], wide // 2
    part = nloc // Y
    half = nloc // piece
    rows = pl.ds(pl.multiple_of(lax.rem(place[0], half) * piece, piece), piece)
    first = place[0] < half

    def masked(k, axis, x):
        at = lax.broadcasted_iota(jnp.int32, (rank, 1) if axis == 0 else (1, rank), axis)
        cuts = [lax.slice_in_dim(x, t * rank, (t + 1) * rank, axis=axis) for t in range(tiles)]
        return jnp.concatenate([jnp.where(at < ranks[k, t], cut, 0.0) for t, cut in enumerate(cuts)], axis)

    for d, v in enumerate((va, vb, vc, vd)):
        source = lax.rem(place[3] + Y - d, Y)
        block[pl.ds(pl.multiple_of(source * part, part), part), :] = v[...]
    v0 = jnp.concatenate([block[:, t * wide : t * wide + rank] for t in range(tiles)], 1)
    v1 = jnp.concatenate([block[:, t * wide + rank : (t + 1) * wide] for t in range(tiles)], 1)
    w = masked(0, 0, dot(v0, diag[0], 0, 1)).astype(BF16)
    wt[...] = w
    lt[...] = dot(w, diag[1], 1, 1).astype(BF16)
    rt[...] = masked(1, 0, dot(v1, diag[2], 0, 1)).astype(BF16)
    top = masked(0, 1, dot(diag[0, rows, :], v0, 1, 0))
    low = dot(diag[1, rows, :], w, 1, 1)
    side = masked(1, 1, dot(diag[2, rows, :], v1, 1, 0))
    left = jnp.where(first, top, low).astype(BF16)
    right = jnp.where(first, 0.0, side).astype(BF16)
    for t in range(tiles):
        cut = slice(t * rank, (t + 1) * rank)
        share[t, :, :rank] = left[:, cut]
        share[t, :, rank:] = right[:, cut]


def tile_cores(place, diag, cuts, wt, lt, rt, cores, column, wc, lrc):
    step = pl.program_id(0)
    some, rank = cores.shape[0], wc.shape[1]

    @pl.when(step == 0)
    def _():
        rows = cuts.shape[1] // Y
        for y in range(Y):
            for p in range(cuts.shape[0]):
                at = (y * cuts.shape[0] + p) * rows
                column[at : at + rows, :] = cuts[p, y * rows : (y + 1) * rows, :]
        w = dot(diag[0], column[:, :rank], 1, 0).astype(BF16)
        wc[...] = w
        lrc[:, :rank] = dot(diag[1], w, 1, 0).astype(BF16)
        lrc[:, rank:] = dot(diag[2], column[:, rank:], 1, 0).astype(BF16)

    both = dot(lt[...], lrc[...], 1, 0)
    corner = dot(wt[...], wc[...], 1, 0)
    below = dot(rt[...], lrc[...], 1, 0)
    for t in range(some):
        cut = slice(t * rank, (t + 1) * rank)
        active = (some * step + t) * place[2] + place[1] > place[0]
        cores[t, :rank, :rank] = jnp.where(active, both[cut, :rank] + corner[cut], 0.0)
        cores[t, :rank, rank:] = jnp.where(active, both[cut, rank:], 0.0)
        cores[t, rank:, :] = jnp.where(active, below[cut], 0.0)


def shards(diag_factors, panel_v, ranks):
    tiles, pair, mine, rank = panel_v.shape
    nrow = lax.axis_size("row")
    ncol = lax.axis_size("col")
    prow = lax.axis_index("row")
    qcol = lax.axis_index("col")
    along_z = [[y * Z + z for z in range(Z)] for y in range(Y)]
    across = [[(p * Y + y) * Z + z for p in range(nrow) for y in range(Y)] for z in range(Z)]
    wide = pair * rank
    ycol, zcol = qcol // Z, qcol % Z
    local = [(y * Z + zcol) // nrow for y in range(Y)]
    place = jnp.stack([qcol, prow, jnp.int32(nrow), ycol] + local + [zcol % nrow]).astype(jnp.int32)
    flat = panel_v.transpose(2, 0, 1, 3).reshape(mine, tiles * wide)
    slab = lax.all_gather(flat, "col", axis=0, tiled=True, axis_index_groups=along_z)
    parts = [slab] + [
        lax.ppermute(slab, "col", [(y * Z + z, (y + d) % Y * Z + z) for y in range(Y) for z in range(Z)])
        for d in range(1, Y)
    ]
    nloc = Y * slab.shape[0]
    rows = slab.shape[0] // nrow

    def of(y):
        return pl.BlockSpec((slab.shape[0], wide), lambda i, where: (0, where[4 + y]))

    picked = pl.pallas_call(
        pick_tiles,
        grid_spec=pltpu.PrefetchScalarGridSpec(
            num_scalar_prefetch=1,
            grid=(1,),
            in_specs=[pl.BlockSpec(memory_space=pltpu.SMEM)] + [of(y) for y in range(Y)],
            out_specs=pl.BlockSpec((nrow, Y, rows, wide), lambda i, where: (0, 0, 0, 0)),
        ),
        out_shape=jax.ShapeDtypeStruct((nrow, Y, rows, wide), BF16),
        compiler_params=pltpu.CompilerParams(vmem_limit_bytes=4 << 20),
        name="pick_tiles",
    )(place, pltpu.with_memory_space_constraint(ranks.T, pltpu.HBM), *[slab] * Y)
    picked = picked.reshape(nrow * Y, rows, wide)
    cut = lax.all_to_all(picked, ("row", "col"), 0, 0, axis_index_groups=across)
    sent = pl.pallas_call(
        spread_cut,
        grid_spec=pltpu.PrefetchScalarGridSpec(
            num_scalar_prefetch=1,
            grid=(1,),
            in_specs=[pl.BlockSpec((Y, rows, wide), lambda i, where: (where[8], 0, 0))],
            out_specs=pl.BlockSpec((nrow, Y, rows, wide), lambda i, where: (0, 0, 0, 0)),
        ),
        out_shape=jax.ShapeDtypeStruct((nrow, Y, rows, wide), BF16),
        compiler_params=pltpu.CompilerParams(vmem_limit_bytes=4 << 20),
        cost_estimate=pl.CostEstimate(flops=0, bytes_accessed=1 << 20, transcendentals=0),
        name="spread_cut",
    )(place, cut)
    cuts = lax.all_to_all(sent.reshape(nrow, Y * rows, wide), "row", 0, 0)

    some = tiles // 2
    scalars = pl.BlockSpec(memory_space=pltpu.SMEM)
    matrices = pl.BlockSpec(diag_factors.shape, lambda i: (0, 0, 0))
    turned = pl.BlockSpec((some * rank, nloc), lambda i: (i, 0))
    full = pl.BlockSpec((tiles * rank, nloc), lambda i: (0, 0))
    lying = pltpu.HBM((tiles * rank, nloc), BF16)
    piece = 2 * nloc // ncol
    limits = pltpu.CompilerParams(vmem_limit_bytes=24 << 20)
    wt, lt, rt, share = pl.pallas_call(
        own_factors,
        grid=(1,),
        in_specs=[scalars, scalars, matrices] + [pl.BlockSpec(slab.shape, lambda i: (0, 0))] * Y,
        out_specs=[full] * 3 + [pl.BlockSpec((tiles, piece, wide), lambda i: (0, 0, 0))],
        out_shape=[lying] * 3 + [jax.ShapeDtypeStruct((tiles, piece, wide), BF16)],
        scratch_shapes=[pltpu.VMEM((nloc, tiles * wide), BF16)],
        compiler_params=limits,
        cost_estimate=pl.CostEstimate(flops=8 * 10**9, bytes_accessed=8 << 20, transcendentals=0),
        name="own_factors",
    )(place, ranks.T, diag_factors, *parts)
    cores = pl.pallas_call(
        tile_cores,
        grid=(tiles // some,),
        in_specs=[scalars, matrices, pl.BlockSpec(cuts.shape, lambda i: (0, 0, 0))] + [turned] * 3,
        out_specs=pl.BlockSpec((some, wide, wide), lambda i: (i, 0, 0)),
        out_shape=jax.ShapeDtypeStruct((tiles, wide, wide), jnp.float32),
        scratch_shapes=[pltpu.VMEM((nloc, n), BF16) for n in (wide, rank, wide)],
        compiler_params=limits,
        cost_estimate=pl.CostEstimate(flops=2 * 10**9, bytes_accessed=7 << 20, transcendentals=0),
        name="tile_cores",
    )(place, diag_factors, cuts, *[pltpu.with_memory_space_constraint(a, pltpu.HBM) for a in (wt, lt, rt)])
    return share, cores[:, None]


def solution(mesh):
    placed = (P(), P("row", None, "col", None), P("row", None))
    return jax.shard_map(
        shards,
        mesh=mesh,
        in_specs=placed,
        out_specs=(P("row", "col", None), P("row", "col", None, None)),
        check_vma=False,
    )
```

```python
import jax
import jax.numpy as jnp
from jax import lax
from jax.experimental import pallas as pl
from jax.experimental.pallas import tpu as pltpu
from jax.sharding import PartitionSpec as P

Y = 4
Z = 16
BF16 = jnp.bfloat16


def dot(a, b, ca, cb):
    return lax.dot_general(a, b, (((ca,), (cb,)), ((), ())), preferred_element_type=jnp.float32)


def pick_tiles(place, ranks, ta, tb, tc, td, picked):
    rank = picked.shape[3] // 2
    lane = lax.broadcasted_iota(jnp.int32, (1, 2 * rank), 1)
    for y, tile in enumerate((ta, tb, tc, td)):
        at = place[4 + y]
        keep = lane < jnp.where(lane < rank, ranks[0, at], ranks[1, at] + rank)
        kept = jnp.where(keep, tile[...].astype(jnp.float32), 0.0).astype(BF16)
        picked[:, y] = kept.reshape(picked.shape[0], picked.shape[2], picked.shape[3])


def spread_cut(place, cut, sent):
    for p in range(sent.shape[0]):
        sent[p] = cut[...]


def own_factors(place, ranks, diag, va, vb, vc, vd, wt, lt, rt, share, block):
    tiles, piece, wide = share.shape
    nloc, rank = block.shape[0], wide // 2
    part = nloc // Y
    half = nloc // piece
    rows = pl.ds(pl.multiple_of(lax.rem(place[0], half) * piece, piece), piece)
    first = place[0] < half

    def masked(k, axis, x):
        at = lax.broadcasted_iota(jnp.int32, (rank, 1) if axis == 0 else (1, rank), axis)
        cuts = [lax.slice_in_dim(x, t * rank, (t + 1) * rank, axis=axis) for t in range(tiles)]
        return jnp.concatenate([jnp.where(at < ranks[k, t], cut, 0.0) for t, cut in enumerate(cuts)], axis)

    for d, v in enumerate((va, vb, vc, vd)):
        source = lax.rem(place[3] + Y - d, Y)
        block[pl.ds(pl.multiple_of(source * part, part), part), :] = v[...]
    v0 = jnp.concatenate([block[:, t * wide : t * wide + rank] for t in range(tiles)], 1)
    v1 = jnp.concatenate([block[:, t * wide + rank : (t + 1) * wide] for t in range(tiles)], 1)
    w = masked(0, 0, dot(v0, diag[0], 0, 1)).astype(BF16)
    wt[...] = w
    lt[...] = dot(w, diag[1], 1, 1).astype(BF16)
    rt[...] = masked(1, 0, dot(v1, diag[2], 0, 1)).astype(BF16)
    top = masked(0, 1, dot(diag[0, rows, :], v0, 1, 0))
    low = dot(diag[1, rows, :], w, 1, 1)
    side = masked(1, 1, dot(diag[2, rows, :], v1, 1, 0))
    left = jnp.where(first, top, low).astype(BF16)
    right = jnp.where(first, 0.0, side).astype(BF16)
    for t in range(tiles):
        cut = slice(t * rank, (t + 1) * rank)
        share[t, :, :rank] = left[:, cut]
        share[t, :, rank:] = right[:, cut]


def tile_cores(place, diag, cuts, wt, lt, rt, cores, column, wc, lrc):
    step = pl.program_id(0)
    some, rank = cores.shape[0], wc.shape[1]

    @pl.when(step == 0)
    def _():
        rows = cuts.shape[1] // Y
        for y in range(Y):
            for p in range(cuts.shape[0]):
                at = (y * cuts.shape[0] + p) * rows
                column[at : at + rows, :] = cuts[p, y * rows : (y + 1) * rows, :]
        w = dot(diag[0], column[:, :rank], 1, 0).astype(BF16)
        wc[...] = w
        lrc[:, :rank] = dot(diag[1], w, 1, 0).astype(BF16)
        lrc[:, rank:] = dot(diag[2], column[:, rank:], 1, 0).astype(BF16)

    both = dot(lt[...], lrc[...], 1, 0)
    corner = dot(wt[...], wc[...], 1, 0)
    below = dot(rt[...], lrc[...], 1, 0)
    for t in range(some):
        cut = slice(t * rank, (t + 1) * rank)
        active = (some * step + t) * place[2] + place[1] > place[0]
        cores[t, :rank, :rank] = jnp.where(active, both[cut, :rank] + corner[cut], 0.0)
        cores[t, :rank, rank:] = jnp.where(active, both[cut, rank:], 0.0)
        cores[t, rank:, :] = jnp.where(active, below[cut], 0.0)


def shards(diag_factors, panel_v, ranks):
    tiles, pair, mine, rank = panel_v.shape
    nrow = lax.axis_size("row")
    ncol = lax.axis_size("col")
    prow = lax.axis_index("row")
    qcol = lax.axis_index("col")
    along_z = [[y * Z + z for z in range(Z)] for y in range(Y)]
    across = [[(p * Y + y) * Z + z for p in range(nrow) for y in range(Y)] for z in range(Z)]
    wide = pair * rank
    ycol, zcol = qcol // Z, qcol % Z
    local = [(y * Z + zcol) // nrow for y in range(Y)]
    place = jnp.stack([qcol, prow, jnp.int32(nrow), ycol] + local + [zcol % nrow]).astype(jnp.int32)
    flat = panel_v.transpose(2, 0, 1, 3).reshape(mine, tiles * wide)
    slab = lax.all_gather(flat, "col", axis=0, tiled=True, axis_index_groups=along_z)
    parts = [slab] + [
        lax.ppermute(slab, "col", [(y * Z + z, (y + d) % Y * Z + z) for y in range(Y) for z in range(Z)])
        for d in range(1, Y)
    ]
    nloc = Y * slab.shape[0]
    rows = slab.shape[0] // nrow

    def of(y):
        return pl.BlockSpec((slab.shape[0], wide), lambda i, where: (0, where[4 + y]))

    picked = pl.pallas_call(
        pick_tiles,
        grid_spec=pltpu.PrefetchScalarGridSpec(
            num_scalar_prefetch=1,
            grid=(1,),
            in_specs=[pl.BlockSpec(memory_space=pltpu.SMEM)] + [of(y) for y in range(Y)],
            out_specs=pl.BlockSpec((nrow, Y, rows, wide), lambda i, where: (0, 0, 0, 0)),
        ),
        out_shape=jax.ShapeDtypeStruct((nrow, Y, rows, wide), BF16),
        compiler_params=pltpu.CompilerParams(vmem_limit_bytes=4 << 20),
        name="pick_tiles",
    )(place, pltpu.with_memory_space_constraint(ranks.T, pltpu.HBM), *[slab] * Y)
    picked = picked.reshape(nrow * Y, rows, wide)
    cut = lax.all_to_all(picked, ("row", "col"), 0, 0, axis_index_groups=across)
    cut, parts[2], parts[1] = lax.optimization_barrier((cut, parts[2], parts[1]))
    sent = pl.pallas_call(
        spread_cut,
        grid_spec=pltpu.PrefetchScalarGridSpec(
            num_scalar_prefetch=1,
            grid=(1,),
            in_specs=[pl.BlockSpec((Y, rows, wide), lambda i, where: (where[8], 0, 0))],
            out_specs=pl.BlockSpec((nrow, Y, rows, wide), lambda i, where: (0, 0, 0, 0)),
        ),
        out_shape=jax.ShapeDtypeStruct((nrow, Y, rows, wide), BF16),
        compiler_params=pltpu.CompilerParams(vmem_limit_bytes=4 << 20),
        cost_estimate=pl.CostEstimate(flops=20 * 10**9, bytes_accessed=1 << 20, transcendentals=0),
        name="spread_cut",
    )(place, cut)
    cuts = lax.all_to_all(sent.reshape(nrow, Y * rows, wide), "row", 0, 0)

    some = tiles // 2
    scalars = pl.BlockSpec(memory_space=pltpu.SMEM)
    matrices = pl.BlockSpec(diag_factors.shape, lambda i: (0, 0, 0))
    turned = pl.BlockSpec((some * rank, nloc), lambda i: (i, 0))
    full = pl.BlockSpec((tiles * rank, nloc), lambda i: (0, 0))
    lying = pltpu.HBM((tiles * rank, nloc), BF16)
    piece = 2 * nloc // ncol
    limits = pltpu.CompilerParams(vmem_limit_bytes=24 << 20)
    wt, lt, rt, share = pl.pallas_call(
        own_factors,
        grid=(1,),
        in_specs=[scalars, scalars, matrices] + [pl.BlockSpec(slab.shape, lambda i: (0, 0))] * Y,
        out_specs=[full] * 3 + [pl.BlockSpec((tiles, piece, wide), lambda i: (0, 0, 0))],
        out_shape=[lying] * 3 + [jax.ShapeDtypeStruct((tiles, piece, wide), BF16)],
        scratch_shapes=[pltpu.VMEM((nloc, tiles * wide), BF16)],
        compiler_params=limits,
        cost_estimate=pl.CostEstimate(flops=8 * 10**9, bytes_accessed=8 << 20, transcendentals=0),
        name="own_factors",
    )(place, ranks.T, diag_factors, *parts)
    cores = pl.pallas_call(
        tile_cores,
        grid=(tiles // some,),
        in_specs=[scalars, matrices, pl.BlockSpec(cuts.shape, lambda i: (0, 0, 0))] + [turned] * 3,
        out_specs=pl.BlockSpec((some, wide, wide), lambda i: (i, 0, 0)),
        out_shape=jax.ShapeDtypeStruct((tiles, wide, wide), jnp.float32),
        scratch_shapes=[pltpu.VMEM((nloc, n), BF16) for n in (wide, rank, wide)],
        compiler_params=limits,
        cost_estimate=pl.CostEstimate(flops=2 * 10**9, bytes_accessed=7 << 20, transcendentals=0),
        name="tile_cores",
    )(place, diag_factors, cuts, *[pltpu.with_memory_space_constraint(a, pltpu.HBM) for a in (wt, lt, rt)])
    return share, cores[:, None]


def solution(mesh):
    placed = (P(), P("row", None, "col", None), P("row", None))
    return jax.shard_map(
        shards,
        mesh=mesh,
        in_specs=placed,
        out_specs=(P("row", "col", None), P("row", "col", None, None)),
        check_vma=False,
    )
```

```python
import jax
import jax.numpy as jnp
from jax import lax
from jax.experimental import pallas as pl
from jax.experimental.pallas import tpu as pltpu
from jax.sharding import PartitionSpec as P

Y = 4
Z = 16
BF16 = jnp.bfloat16


def dot(a, b, ca, cb):
    return lax.dot_general(a, b, (((ca,), (cb,)), ((), ())), preferred_element_type=jnp.float32)


def lower(v, a):
    half = a.shape[0] // 2
    return jnp.concatenate([dot(v[:half], a[:half, :half], 0, 1), dot(v, a[half:], 0, 1)], 1)


def lower_times(a, v):
    half = a.shape[0] // 2
    return jnp.concatenate([dot(a[:half, :half], v[:half], 1, 0), dot(a[half:], v, 1, 0)], 0)


def pick_tiles(place, ranks, ta, tb, tc, td, picked):
    rank = picked.shape[3] // 2
    lane = lax.broadcasted_iota(jnp.int32, (1, 2 * rank), 1)
    for y, tile in enumerate((ta, tb, tc, td)):
        at = place[4 + y]
        keep = lane < jnp.where(lane < rank, ranks[0, at], ranks[1, at] + rank)
        kept = jnp.where(keep, tile[...].astype(jnp.float32), 0.0).astype(BF16)
        picked[:, y] = kept.reshape(picked.shape[0], picked.shape[2], picked.shape[3])


def spread_cut(place, cut, sent):
    for p in range(sent.shape[0]):
        sent[p] = cut[...]


def own_factors(place, ranks, diag, va, vb, vc, vd, wt, lt, rt, share, block):
    tiles, piece, wide = share.shape
    nloc, rank = block.shape[0], wide // 2
    part = nloc // Y
    half = nloc // piece
    rows = pl.ds(pl.multiple_of(lax.rem(place[0], half) * piece, piece), piece)
    first = place[0] < half

    def masked(k, axis, x):
        at = lax.broadcasted_iota(jnp.int32, (rank, 1) if axis == 0 else (1, rank), axis)
        cuts = [lax.slice_in_dim(x, t * rank, (t + 1) * rank, axis=axis) for t in range(tiles)]
        return jnp.concatenate([jnp.where(at < ranks[k, t], cut, 0.0) for t, cut in enumerate(cuts)], axis)

    for d, v in enumerate((va, vb, vc, vd)):
        source = lax.rem(place[3] + Y - d, Y)
        block[pl.ds(pl.multiple_of(source * part, part), part), :] = v[...]
    v0 = jnp.concatenate([block[:, t * wide : t * wide + rank] for t in range(tiles)], 1)
    v1 = jnp.concatenate([block[:, t * wide + rank : (t + 1) * wide] for t in range(tiles)], 1)
    w = masked(0, 0, lower(v0, diag[0])).astype(BF16)
    wt[...] = w
    lt[...] = dot(w, diag[1], 1, 1).astype(BF16)
    rt[...] = masked(1, 0, lower(v1, diag[2])).astype(BF16)
    top = masked(0, 1, dot(diag[0, rows, :], v0, 1, 0))
    low = dot(diag[1, rows, :], w, 1, 1)
    side = masked(1, 1, dot(diag[2, rows, :], v1, 1, 0))
    left = jnp.where(first, top, low).astype(BF16)
    right = jnp.where(first, 0.0, side).astype(BF16)
    for t in range(tiles):
        cut = slice(t * rank, (t + 1) * rank)
        share[t, :, :rank] = left[:, cut]
        share[t, :, rank:] = right[:, cut]


def tile_cores(place, diag, cuts, wt, lt, rt, cores, column, wc, lrc):
    step = pl.program_id(0)
    some, rank = cores.shape[0], wc.shape[1]

    @pl.when(step == 0)
    def _():
        rows = cuts.shape[1] // Y
        for y in range(Y):
            for p in range(cuts.shape[0]):
                at = (y * cuts.shape[0] + p) * rows
                column[at : at + rows, :] = cuts[p, y * rows : (y + 1) * rows, :]
        w = lower_times(diag[0], column[:, :rank]).astype(BF16)
        wc[...] = w
        lrc[:, :rank] = dot(diag[1], w, 1, 0).astype(BF16)
        lrc[:, rank:] = lower_times(diag[2], column[:, rank:]).astype(BF16)

    both = dot(lt[...], lrc[...], 1, 0)
    corner = dot(wt[...], wc[...], 1, 0)
    below = dot(rt[...], lrc[...], 1, 0)
    for t in range(some):
        cut = slice(t * rank, (t + 1) * rank)
        active = (some * step + t) * place[2] + place[1] > place[0]
        cores[t, :rank, :rank] = jnp.where(active, both[cut, :rank] + corner[cut], 0.0)
        cores[t, :rank, rank:] = jnp.where(active, both[cut, rank:], 0.0)
        cores[t, rank:, :] = jnp.where(active, below[cut], 0.0)


def shards(diag_factors, panel_v, ranks):
    tiles, pair, mine, rank = panel_v.shape
    nrow = lax.axis_size("row")
    ncol = lax.axis_size("col")
    prow = lax.axis_index("row")
    qcol = lax.axis_index("col")
    along_z = [[y * Z + z for z in range(Z)] for y in range(Y)]
    across = [[(p * Y + y) * Z + z for p in range(nrow) for y in range(Y)] for z in range(Z)]
    wide = pair * rank
    ycol, zcol = qcol // Z, qcol % Z
    local = [(y * Z + zcol) // nrow for y in range(Y)]
    place = jnp.stack([qcol, prow, jnp.int32(nrow), ycol] + local + [zcol % nrow]).astype(jnp.int32)
    flat = panel_v.transpose(2, 0, 1, 3).reshape(mine, tiles * wide)
    slab = lax.all_gather(flat, "col", axis=0, tiled=True, axis_index_groups=along_z)
    parts = [slab] + [
        lax.ppermute(slab, "col", [(y * Z + z, (y + d) % Y * Z + z) for y in range(Y) for z in range(Z)])
        for d in range(1, Y)
    ]
    nloc = Y * slab.shape[0]
    rows = slab.shape[0] // nrow

    def of(y):
        return pl.BlockSpec((slab.shape[0], wide), lambda i, where: (0, where[4 + y]))

    picked = pl.pallas_call(
        pick_tiles,
        grid_spec=pltpu.PrefetchScalarGridSpec(
            num_scalar_prefetch=1,
            grid=(1,),
            in_specs=[pl.BlockSpec(memory_space=pltpu.SMEM)] + [of(y) for y in range(Y)],
            out_specs=pl.BlockSpec((nrow, Y, rows, wide), lambda i, where: (0, 0, 0, 0)),
        ),
        out_shape=jax.ShapeDtypeStruct((nrow, Y, rows, wide), BF16),
        compiler_params=pltpu.CompilerParams(vmem_limit_bytes=4 << 20),
        name="pick_tiles",
    )(place, pltpu.with_memory_space_constraint(ranks.T, pltpu.HBM), *[slab] * Y)
    picked = picked.reshape(nrow * Y, rows, wide)
    cut = lax.all_to_all(picked, ("row", "col"), 0, 0, axis_index_groups=across)
    cut, parts[2], parts[1] = lax.optimization_barrier((cut, parts[2], parts[1]))
    sent = pl.pallas_call(
        spread_cut,
        grid_spec=pltpu.PrefetchScalarGridSpec(
            num_scalar_prefetch=1,
            grid=(1,),
            in_specs=[pl.BlockSpec((Y, rows, wide), lambda i, where: (where[8], 0, 0))],
            out_specs=pl.BlockSpec((nrow, Y, rows, wide), lambda i, where: (0, 0, 0, 0)),
        ),
        out_shape=jax.ShapeDtypeStruct((nrow, Y, rows, wide), BF16),
        compiler_params=pltpu.CompilerParams(vmem_limit_bytes=4 << 20),
        cost_estimate=pl.CostEstimate(flops=20 * 10**9, bytes_accessed=1 << 20, transcendentals=0),
        name="spread_cut",
    )(place, cut)
    cuts = lax.all_to_all(sent.reshape(nrow, Y * rows, wide), "row", 0, 0)

    some = tiles // 2
    scalars = pl.BlockSpec(memory_space=pltpu.SMEM)
    matrices = pl.BlockSpec(diag_factors.shape, lambda i: (0, 0, 0))
    turned = pl.BlockSpec((some * rank, nloc), lambda i: (i, 0))
    full = pl.BlockSpec((tiles * rank, nloc), lambda i: (0, 0))
    lying = pltpu.HBM((tiles * rank, nloc), BF16)
    piece = 2 * nloc // ncol
    limits = pltpu.CompilerParams(vmem_limit_bytes=24 << 20)
    wt, lt, rt, share = pl.pallas_call(
        own_factors,
        grid=(1,),
        in_specs=[scalars, scalars, matrices] + [pl.BlockSpec(slab.shape, lambda i: (0, 0))] * Y,
        out_specs=[full] * 3 + [pl.BlockSpec((tiles, piece, wide), lambda i: (0, 0, 0))],
        out_shape=[lying] * 3 + [jax.ShapeDtypeStruct((tiles, piece, wide), BF16)],
        scratch_shapes=[pltpu.VMEM((nloc, tiles * wide), BF16)],
        compiler_params=limits,
        cost_estimate=pl.CostEstimate(flops=8 * 10**9, bytes_accessed=8 << 20, transcendentals=0),
        name="own_factors",
    )(place, ranks.T, diag_factors, *parts)
    cores = pl.pallas_call(
        tile_cores,
        grid=(tiles // some,),
        in_specs=[scalars, matrices, pl.BlockSpec(cuts.shape, lambda i: (0, 0, 0))] + [turned] * 3,
        out_specs=pl.BlockSpec((some, wide, wide), lambda i: (i, 0, 0)),
        out_shape=jax.ShapeDtypeStruct((tiles, wide, wide), jnp.float32),
        scratch_shapes=[pltpu.VMEM((nloc, n), BF16) for n in (wide, rank, wide)],
        compiler_params=limits,
        cost_estimate=pl.CostEstimate(flops=2 * 10**9, bytes_accessed=7 << 20, transcendentals=0),
        name="tile_cores",
    )(place, diag_factors, cuts, *[pltpu.with_memory_space_constraint(a, pltpu.HBM) for a in (wt, lt, rt)])
    return share, cores[:, None]


def solution(mesh):
    placed = (P(), P("row", None, "col", None), P("row", None))
    return jax.shard_map(
        shards,
        mesh=mesh,
        in_specs=placed,
        out_specs=(P("row", "col", None), P("row", "col", None, None)),
        check_vma=False,
    )
```

```python
import jax
import jax.numpy as jnp
from jax import lax
from jax.experimental import pallas as pl
from jax.experimental.pallas import tpu as pltpu
from jax.sharding import PartitionSpec as P

Y = 4
Z = 16
BF16 = jnp.bfloat16


def dot(a, b, ca, cb):
    return lax.dot_general(a, b, (((ca,), (cb,)), ((), ())), preferred_element_type=jnp.float32)


def lower(v, a):
    half = a.shape[0] // 2
    return jnp.concatenate([dot(v[:half], a[:half, :half], 0, 1), dot(v, a[half:], 0, 1)], 1)


def lower_times(a, v):
    half = a.shape[0] // 2
    return jnp.concatenate([dot(a[:half, :half], v[:half], 1, 0), dot(a[half:], v, 1, 0)], 0)


def pick_tiles(place, ranks, ta, tb, tc, td, picked):
    rank = picked.shape[3] // 2
    lane = lax.broadcasted_iota(jnp.int32, (1, 2 * rank), 1)
    for y, tile in enumerate((ta, tb, tc, td)):
        at = place[4 + y]
        keep = lane < jnp.where(lane < rank, ranks[0, at], ranks[1, at] + rank)
        kept = jnp.where(keep, tile[...].astype(jnp.float32), 0.0).astype(BF16)
        picked[:, y] = kept.reshape(picked.shape[0], picked.shape[2], picked.shape[3])


def spread_cut(place, cut, sent):
    for p in range(sent.shape[0]):
        sent[p] = cut[...]


def own_factors(place, ranks, diag, va, vb, vc, vd, wt, lt, rt, share, block):
    tiles, piece, wide = share.shape
    nloc, rank = block.shape[0], wide // 2
    part = nloc // Y
    half = nloc // piece
    rows = pl.ds(pl.multiple_of(lax.rem(place[0], half) * piece, piece), piece)
    first = place[0] < half

    def masked(k, axis, x):
        at = lax.broadcasted_iota(jnp.int32, (rank, 1) if axis == 0 else (1, rank), axis)
        cuts = [lax.slice_in_dim(x, t * rank, (t + 1) * rank, axis=axis) for t in range(tiles)]
        return jnp.concatenate([jnp.where(at < ranks[k, t], cut, 0.0) for t, cut in enumerate(cuts)], axis)

    for d, v in enumerate((va, vb, vc, vd)):
        source = lax.rem(place[3] + Y - d, Y)
        block[pl.ds(pl.multiple_of(source * part, part), part), :] = v[...]
    v0 = jnp.concatenate([block[:, t * wide : t * wide + rank] for t in range(tiles)], 1)
    v1 = jnp.concatenate([block[:, t * wide + rank : (t + 1) * wide] for t in range(tiles)], 1)
    w = masked(0, 0, lower(v0, diag[0])).astype(BF16)
    wt[...] = w
    lt[...] = dot(w, diag[1], 1, 1).astype(BF16)
    rt[...] = masked(1, 0, lower(v1, diag[2])).astype(BF16)
    top = masked(0, 1, dot(diag[0, rows, :], v0, 1, 0))
    low = dot(diag[1, rows, :], w, 1, 1)
    side = masked(1, 1, dot(diag[2, rows, :], v1, 1, 0))
    left = jnp.where(first, top, low).astype(BF16)
    right = jnp.where(first, 0.0, side).astype(BF16)
    for t in range(tiles):
        cut = slice(t * rank, (t + 1) * rank)
        share[t, :, :rank] = left[:, cut]
        share[t, :, rank:] = right[:, cut]


def tile_cores(place, diag, cuts, wt, lt, rt, cores, column, wc, lrc):
    step = pl.program_id(0)
    some, rank = cores.shape[0], wc.shape[1]

    @pl.when(step == 0)
    def _():
        rows = cuts.shape[1] // Y
        for y in range(Y):
            for p in range(cuts.shape[0]):
                at = (y * cuts.shape[0] + p) * rows
                column[at : at + rows, :] = cuts[p, y * rows : (y + 1) * rows, :]
        w = lower_times(diag[0], column[:, :rank]).astype(BF16)
        wc[...] = w
        lrc[:, :rank] = dot(diag[1], w, 1, 0).astype(BF16)
        lrc[:, rank:] = lower_times(diag[2], column[:, rank:]).astype(BF16)

    both = dot(lt[...], lrc[...], 1, 0)
    corner = dot(wt[...], wc[...], 1, 0)
    below = dot(rt[...], lrc[...], 1, 0)
    for t in range(some):
        cut = slice(t * rank, (t + 1) * rank)
        active = (some * step + t) * place[2] + place[1] > place[0]
        cores[t, :rank, :rank] = jnp.where(active, both[cut, :rank] + corner[cut], 0.0)
        cores[t, :rank, rank:] = jnp.where(active, both[cut, rank:], 0.0)
        cores[t, rank:, :] = jnp.where(active, below[cut], 0.0)


def shards(diag_factors, panel_v, ranks):
    tiles, pair, mine, rank = panel_v.shape
    nrow = lax.axis_size("row")
    ncol = lax.axis_size("col")
    prow = lax.axis_index("row")
    qcol = lax.axis_index("col")
    along_z = [[y * Z + z for z in range(Z)] for y in range(Y)]
    across = [[(p * Y + y) * Z + z for p in range(nrow) for y in range(Y)] for z in range(Z)]
    wide = pair * rank
    ycol, zcol = qcol // Z, qcol % Z
    local = [(y * Z + zcol) // nrow for y in range(Y)]
    place = jnp.stack([qcol, prow, jnp.int32(nrow), ycol] + local + [zcol % nrow]).astype(jnp.int32)
    flat = panel_v.transpose(2, 0, 1, 3).reshape(mine, tiles * wide)
    slab = lax.all_gather(flat, "col", axis=0, tiled=True, axis_index_groups=along_z)
    parts = [slab] + [
        lax.ppermute(slab, "col", [(y * Z + z, (y + d) % Y * Z + z) for y in range(Y) for z in range(Z)])
        for d in range(1, Y)
    ]
    nloc = Y * slab.shape[0]
    rows = slab.shape[0] // nrow

    def of(y):
        return pl.BlockSpec((slab.shape[0], wide), lambda i, where: (0, where[4 + y]))

    picked = pl.pallas_call(
        pick_tiles,
        grid_spec=pltpu.PrefetchScalarGridSpec(
            num_scalar_prefetch=1,
            grid=(1,),
            in_specs=[pl.BlockSpec(memory_space=pltpu.SMEM)] + [of(y) for y in range(Y)],
            out_specs=pl.BlockSpec((nrow, Y, rows, wide), lambda i, where: (0, 0, 0, 0)),
        ),
        out_shape=jax.ShapeDtypeStruct((nrow, Y, rows, wide), BF16),
        compiler_params=pltpu.CompilerParams(vmem_limit_bytes=4 << 20),
        name="pick_tiles",
    )(place, pltpu.with_memory_space_constraint(ranks.T, pltpu.HBM), *[slab] * Y)
    picked = picked.reshape(nrow * Y, rows, wide)
    cut = lax.all_to_all(picked, ("row", "col"), 0, 0, axis_index_groups=across)
    cut, parts[2] = lax.optimization_barrier((cut, parts[2]))
    sent = pl.pallas_call(
        spread_cut,
        grid_spec=pltpu.PrefetchScalarGridSpec(
            num_scalar_prefetch=1,
            grid=(1,),
            in_specs=[pl.BlockSpec((Y, rows, wide), lambda i, where: (where[8], 0, 0))],
            out_specs=pl.BlockSpec((nrow, Y, rows, wide), lambda i, where: (0, 0, 0, 0)),
        ),
        out_shape=jax.ShapeDtypeStruct((nrow, Y, rows, wide), BF16),
        compiler_params=pltpu.CompilerParams(vmem_limit_bytes=4 << 20),
        cost_estimate=pl.CostEstimate(flops=20 * 10**9, bytes_accessed=1 << 20, transcendentals=0),
        name="spread_cut",
    )(place, cut)
    cuts = lax.all_to_all(sent.reshape(nrow, Y * rows, wide), "row", 0, 0)

    some = tiles // 2
    scalars = pl.BlockSpec(memory_space=pltpu.SMEM)
    matrices = pl.BlockSpec(diag_factors.shape, lambda i: (0, 0, 0))
    turned = pl.BlockSpec((some * rank, nloc), lambda i: (i, 0))
    full = pl.BlockSpec((tiles * rank, nloc), lambda i: (0, 0))
    lying = pltpu.HBM((tiles * rank, nloc), BF16)
    piece = 2 * nloc // ncol
    limits = pltpu.CompilerParams(vmem_limit_bytes=24 << 20)
    wt, lt, rt, share = pl.pallas_call(
        own_factors,
        grid=(1,),
        in_specs=[scalars, scalars, matrices] + [pl.BlockSpec(slab.shape, lambda i: (0, 0))] * Y,
        out_specs=[full] * 3 + [pl.BlockSpec((tiles, piece, wide), lambda i: (0, 0, 0))],
        out_shape=[lying] * 3 + [jax.ShapeDtypeStruct((tiles, piece, wide), BF16)],
        scratch_shapes=[pltpu.VMEM((nloc, tiles * wide), BF16)],
        compiler_params=limits,
        cost_estimate=pl.CostEstimate(flops=8 * 10**9, bytes_accessed=8 << 20, transcendentals=0),
        name="own_factors",
    )(place, ranks.T, diag_factors, *parts)
    cores = pl.pallas_call(
        tile_cores,
        grid=(tiles // some,),
        in_specs=[scalars, matrices, pl.BlockSpec(cuts.shape, lambda i: (0, 0, 0))] + [turned] * 3,
        out_specs=pl.BlockSpec((some, wide, wide), lambda i: (i, 0, 0)),
        out_shape=jax.ShapeDtypeStruct((tiles, wide, wide), jnp.float32),
        scratch_shapes=[pltpu.VMEM((nloc, n), BF16) for n in (wide, rank, wide)],
        compiler_params=limits,
        cost_estimate=pl.CostEstimate(flops=2 * 10**9, bytes_accessed=7 << 20, transcendentals=0),
        name="tile_cores",
    )(place, diag_factors, cuts, *[pltpu.with_memory_space_constraint(a, pltpu.HBM) for a in (wt, lt, rt)])
    return share, cores[:, None]


def solution(mesh):
    placed = (P(), P("row", None, "col", None), P("row", None))
    return jax.shard_map(
        shards,
        mesh=mesh,
        in_specs=placed,
        out_specs=(P("row", "col", None), P("row", "col", None, None)),
        check_vma=False,
    )
```
